128 devices in a mesh: row: 8 (over z_lo, y), col: 16 (over x, z_hi, core).
Axes of the slice: x: 4, y: 4, z: 4 (z_hi: 2, z_lo: 2; z = z_hi * 2 + z_lo), core: 2. Of those that a mesh axis runs over, the one named last changes fastest.
Arguments:
- amplitudes: bfloat16 [12288, 8192], P('row', 'col'), may hold values from -6 to 6
- integrals: bfloat16 [8192, 8192], P('row', 'col'), may hold values from -0.09375 to 0.09375
- screen_mask: int32 [96, 64], P('row', 'col'), may hold values from 0 to 1, as said below
- tile_order: int32 [64], replicated, may hold values from 0 to 63, each once
Outputs:
- ladder: float32 [12288, 8192], P('row', 'col')
The draws below stay inside these ranges and needn't reach their ends.
Inputs may be any that keep to these rules, and one draw needn't show every extreme that they name: `screen_mask`: in every aligned block of 12 tile rows by 4 tile columns exactly 24 tiles survive; rows of tiles hold different numbers of them. `tile_order`: each number of 0 to 63 appears once.
All inputs are finite; a program needn't handle non-finite values.
Results may differ from the reference program's by a relative error of at most 0.0003.
Values may be sent and summed in bfloat16 or wider, within the bound.
A program may use at most 256 MiB of HBM per device.

```python
import jax
import jax.numpy as jnp

TILE_PAIRS = 128
TILES_PER_ROW = 12
KTC = 4
CAP = 24
OCCUPIED_TILES = 96
CONTRACT_TILES = 64
OCCUPIED_PAIRS = 12288
NPAIRS = 8192
VIRTUAL_PAIRS = 8192


def draw_screen_mask(key, part):
    first_key, second_key = jax.random.split(jax.random.fold_in(key, 17))
    row_partitions = OCCUPIED_TILES // TILES_PER_ROW
    col_groups = CONTRACT_TILES // KTC
    block_size = TILES_PER_ROW * KTC
    levels = jax.random.randint(first_key, (row_partitions, TILES_PER_ROW, 1, 1), 0, 4)
    rolled = jax.random.randint(second_key, (row_partitions, TILES_PER_ROW, col_groups, KTC), 0, 4)
    scores = levels * 4 + rolled
    blocks = jnp.transpose(scores, (0, 2, 1, 3)).reshape(row_partitions, col_groups, block_size)
    position = jnp.arange(block_size, dtype=jnp.int32)
    distinct = (15 - blocks) * block_size + position
    ranks = jnp.argsort(jnp.argsort(distinct, axis=-1), axis=-1)
    keep_flags = (ranks < CAP).astype(jnp.int32).reshape(row_partitions, col_groups, TILES_PER_ROW, KTC)
    return jnp.transpose(keep_flags, (0, 2, 1, 3)).reshape(OCCUPIED_TILES, CONTRACT_TILES)


def level_of(key, extent, cuts, smallest, high):
    factor_of = 1.0
    for dim, blocks in cuts:
        draws = jax.random.uniform(jax.random.fold_in(jax.random.fold_in(key, 6), dim), (blocks,), jnp.float32, smallest / len(cuts), high / len(cuts))
        factor_of = factor_of * jnp.repeat(jnp.exp(draws), extent[dim] // blocks).reshape((-1,) + (1,) * (len(extent) - 1 - dim))
    return factor_of


def gaussian(rng, shape, deviation, limit, cuts=(), kind=jnp.bfloat16):
    drawn = deviation * jax.random.normal(rng, shape, jnp.float32)
    if cuts:
        drawn = drawn * level_of(rng, shape, cuts, -0.22, 0.18)
    return jnp.clip(drawn, -limit, limit).astype(kind)


def setup_inputs(seed: int = 0) -> dict:
    keys = jax.random.split(jax.random.key(seed), 5)
    return {
        "amplitudes": gaussian(keys[0], (OCCUPIED_PAIRS, VIRTUAL_PAIRS), 1.0, 6.0, ((0, 8), (1, 16))),
        "integrals": gaussian(keys[1], (VIRTUAL_PAIRS, NPAIRS), (VIRTUAL_PAIRS // 2) ** -0.5, 0.09375, ((0, 8), (1, 16))),
        "screen_mask": draw_screen_mask(jax.random.fold_in(keys[4], 71), 0),
        "tile_order": jax.random.permutation(keys[3], CONTRACT_TILES).astype(jnp.int32),
    }


def reference(amplitudes, integrals, screen_mask, tile_order):
    weight_values = screen_mask.astype(jnp.bfloat16)[:, None, :, None]
    screened_tiles = (amplitudes.reshape(OCCUPIED_TILES, TILE_PAIRS, CONTRACT_TILES, TILE_PAIRS) * weight_values).reshape(OCCUPIED_PAIRS, VIRTUAL_PAIRS)
    ordered = jnp.take(integrals.reshape(CONTRACT_TILES, TILE_PAIRS, NPAIRS), tile_order.astype(jnp.int32), axis=0).reshape(VIRTUAL_PAIRS, NPAIRS)
    return jnp.dot(screened_tiles, ordered, preferred_element_type=jnp.float32)
```

```python
import jax
import jax.numpy as jnp
from jax import lax
from jax.experimental import pallas as pl
from jax.experimental.pallas import tpu as pltpu
from jax.sharding import PartitionSpec as P

MESH = pl.DeviceIdType.MESH
T = 128
ROWT, KT, CAP = 12, 4, 24
M = ROWT * T
DEPTH = 8
H = 256
ZERO = CAP
CUT = 5
CHUNK = 768

B_IDS = ("zp", "yp", "ym", "pp", "pm", "fp", "fm", "zhp", "zhm", "gp", "gm")
A_IDS = ("ax+", "ax-", "az", "ac", "bx+", "bx-", "bc", "af+", "af-", "bf+", "bf-",
         "c1", "c2", "c3", "d1", "d2", "d3")
IDS = {}
for _h in (0, 1):
    for _n in B_IDS:
        IDS[(_n, _h)] = len(IDS)
for _n in A_IDS:
    IDS[_n] = len(IDS)
for _n in A_IDS:
    if _n not in ("af-", "bf-"):
        IDS[("m", _n)] = len(IDS)


def kernel(a_in, b_in, mask, order, out, *scratch):
    A = scratch[0:16]
    meta = scratch[16:32]
    (a_loc, dense, b0, b1, acc0, acc1, inv_v, inv_s, nxt, pos, cnt, ss, rs, ls) = scratch[32:]
    B, ACC = (b0, b1), (acc0, acc1)
    row, col = lax.axis_index("row"), lax.axis_index("col")
    y, zl = lax.rem(row, 4), lax.div(row, 4)
    core, zh, x = lax.rem(col, 2), lax.rem(lax.div(col, 2), 2), lax.div(col, 4)

    def at(dx=0, dy=0, dzl=0, dzh=0, dcore=0):
        r = lax.rem(zl + dzl, 2) * 4 + lax.rem(y + dy, 4)
        c = (lax.rem(x + dx, 4) * 2 + lax.rem(zh + dzh, 2)) * 2 + lax.rem(core + dcore, 2)
        return r, c

    up, down, zpart = at(dy=1), at(dy=3), at(dzl=1)
    right, left, hpart, sib = at(dx=1), at(dx=3), at(dzh=1), at(dcore=1)
    peers = (up, down, zpart, right, left, hpart, sib)

    barrier = pltpu.get_barrier_semaphore()
    for p in peers:
        pl.semaphore_signal(barrier, inc=1, device_id=p, device_id_type=MESH)

    local = []
    for k in range(KT):
        local.append(pltpu.make_async_copy(a_in.at[:, :, pl.ds(k * T, T)], a_loc.at[pl.ds(k * ROWT, ROWT)], ls.at[k]))
    for h in (0, 1):
        local.append(pltpu.make_async_copy(b_in.at[:, :, pl.ds(h * H, H)], B[h].at[pl.ds(row * DEPTH, DEPTH)], ls.at[KT + h]))
    for c in local:
        c.start()
    pl.semaphore_wait(barrier, len(peers))

    started = []

    def send(name, src, dst, device):
        i = IDS[name]
        c = pltpu.make_async_remote_copy(src, dst, ss.at[i], rs.at[i], device_id=device, device_id_type=MESH)
        c.start()
        started.append(c)

    def got(name, ref):
        i = IDS[name]
        pltpu.make_async_remote_copy(ref, ref, ss.at[i], rs.at[i], device_id=sib, device_id_type=MESH).wait_recv()

    def rows_of(h, dzl, dy, first=0, count=DEPTH):
        r = lax.rem(zl + dzl, 2) * 4 + lax.rem(y + dy, 4)
        return B[h].at[pl.ds(r * DEPTH + first, count)]

    def b_send(name, h, dzl, dy, device, first=0, count=DEPTH, own=False):
        dst = rows_of(h, dzl, dy, first, count)
        src = b_in.at[:, :, pl.ds(h * H, H)] if own else dst
        send((name, h), src, dst, device)

    HALF = DEPTH // 2
    LANDS = {
        "zp": (1, 0, 0, DEPTH), "yp": (0, 3, 0, DEPTH), "ym": (0, 1, 0, DEPTH),
        "pp": (1, 3, 0, CUT), "pm": (1, 1, DEPTH - CUT, CUT),
        "fp": (0, 2, 0, HALF), "fm": (0, 2, HALF, HALF),
        "zhp": (1, 3, CUT, DEPTH - CUT), "zhm": (1, 1, 0, DEPTH - CUT),
        "gp": (1, 2, 0, HALF), "gm": (1, 2, HALF, HALF),
    }

    def b_got(h, *names):
        for n in names:
            got((n, h), rows_of(h, *LANDS[n]))

    def b_own_y(h):
        b_send("yp", h, 0, 0, up, own=True)
        b_send("ym", h, 0, 0, down, own=True)

    def b_own_z(h):
        b_send("zp", h, 0, 0, zpart, own=True)

    def b_near(h):
        b_got(h, "yp")
        b_send("fp", h, 0, 3, up, 0, HALF)
        b_got(h, "ym")
        b_send("fm", h, 0, 1, down, HALF, HALF)
        b_send("zhp", h, 0, 3, zpart, CUT, DEPTH - CUT)
        b_send("zhm", h, 0, 1, zpart, 0, DEPTH - CUT)

    def b_partner(h):
        b_got(h, "zp")
        b_send("pp", h, 1, 0, up, 0, CUT)
        b_send("pm", h, 1, 0, down, DEPTH - CUT, CUT)

    def b_far(h):
        b_got(h, "pp")
        b_send("gp", h, 1, 3, up, 0, HALF)
        b_got(h, "pm")
        b_send("gm", h, 1, 1, down, HALF, HALF)

    def slot(dzh, dcore, dx):
        return dzh * 8 + dcore * 4 + dx

    A_LANDS = {
        "ax+": (slot(0, 0, 3), 0, CAP), "ax-": (slot(0, 0, 1), 0, CAP),
        "az": (slot(1, 0, 0), 0, CAP), "ac": (slot(0, 1, 0), 0, CAP),
        "bx+": (slot(1, 0, 3), 0, CAP), "bx-": (slot(1, 0, 1), 0, CAP), "bc": (slot(1, 1, 0), 0, CAP),
        "af+": (slot(0, 0, 2), 0, CAP // 2), "af-": (slot(0, 0, 2), CAP // 2, CAP // 2),
        "bf+": (slot(1, 0, 2), 0, CAP // 2), "bf-": (slot(1, 0, 2), CAP // 2, CAP // 2),
        "c1": (slot(0, 1, 1), 0, CAP), "c2": (slot(0, 1, 2), 0, CAP), "c3": (slot(0, 1, 3), 0, CAP),
        "d1": (slot(1, 1, 1), 0, CAP), "d2": (slot(1, 1, 2), 0, CAP), "d3": (slot(1, 1, 3), 0, CAP),
    }

    def a_send(name, src, device):
        s, first, count = A_LANDS[name]
        rows = pl.ds(first, count)
        send(name, A[src].at[rows], A[s].at[rows], device)
        if ("m", name) in IDS:
            send(("m", name), meta[src], meta[s], device)

    def a_got(*names):
        for n in names:
            s, first, count = A_LANDS[n]
            got(n, A[s].at[pl.ds(first, count)])
            if ("m", n) in IDS:
                got(("m", n), meta[s])

    def col_of(g):
        dzh, dcore, dx = lax.div(g, 8), lax.rem(lax.div(g, 4), 2), lax.rem(g, 4)
        return (lax.rem(x + dx, 4) * 2 + lax.rem(zh + dzh, 2)) * 2 + lax.rem(core + dcore, 2)

    def expand(s):
        base = col_of(jnp.int32(s)) * KT

        @pl.loop(0, KT * ROWT)
        def _(t):
            rows = pl.ds(pl.multiple_of(lax.rem(t, ROWT) * T, T), T)
            dense[base + lax.div(t, ROWT), rows, :] = A[s][meta[s][t]]

    def left_part(g):
        c = col_of(g)
        for m in range(M // CHUNK):
            lhs = jnp.concatenate(
                [dense[c * KT + j, pl.ds(m * CHUNK, CHUNK), :] for j in range(KT)], axis=1)
            rhs = jnp.concatenate(
                [b0[order[c * KT + j]] for j in range(KT)], axis=0)
            acc0[pl.ds(m * CHUNK, CHUNK), :] += jnp.dot(lhs, rhs, preferred_element_type=jnp.float32)

    def right_part(g):
        r = lax.rem(zl + lax.div(g, 4), 2) * 4 + lax.rem(y + lax.rem(g, 4), 4)
        for m in range(M // CHUNK):
            for q in (0, 1):
                lhs = jnp.concatenate(
                    [dense[inv_s[0, r * 8 + q * 4 + j], pl.ds(m * CHUNK, CHUNK), :]
                     for j in range(4)], axis=1)
                rhs = b1[pl.ds(r * DEPTH + q * 4, 4)].reshape(4 * T, H)
                acc1[pl.ds(m * CHUNK, CHUNK), :] += jnp.dot(lhs, rhs, preferred_element_type=jnp.float32)

    b_own_y(0)
    b_own_z(0)

    nxt[KT * ROWT] = 0

    @pl.loop(0, KT * ROWT)
    def _(n):
        t = KT * ROWT - 1 - n
        keep = mask[lax.rem(t, ROWT), lax.div(t, ROWT)]
        nxt[t] = keep * t + (1 - keep) * nxt[t + 1]

    cnt[0] = 0

    @pl.loop(0, KT * ROWT)
    def _(t):
        keep = mask[lax.rem(t, ROWT), lax.div(t, ROWT)]
        meta[0][t] = keep * cnt[t] + (1 - keep) * ZERO
        cnt[t + 1] = cnt[t] + keep

    for k in range(KT):
        local[k].wait()
    pos[0] = nxt[0]

    @pl.loop(0, CAP)
    def _(s):
        A[0][s] = a_loc[pos[s]]
        pos[s + 1] = nxt[pos[s] + 1]

    a_send("ax+", 0, right)
    a_send("ax-", 0, left)
    a_send("az", 0, hpart)
    a_send("ac", 0, sib)

    lane = lax.broadcasted_iota(jnp.int32, (8, 128), 1)
    inv_v[...] = jnp.zeros((8, 128), jnp.int32)

    @pl.loop(0, 64)
    def _(k):
        apart = lane - order[k]
        inv_v[...] += (k - inv_v[...]) * (1 - jnp.minimum(jnp.maximum(apart, -apart), 1))

    to_s = pltpu.make_async_copy(inv_v, inv_s, ls.at[KT + 2])
    to_s.start()
    for s in range(16):
        A[s][ZERO] = jnp.zeros((T, T), jnp.bfloat16)
    acc0[...] = jnp.zeros_like(acc0)
    acc1[...] = jnp.zeros_like(acc1)
    expand(0)
    to_s.wait()
    local[KT].wait()
    local[KT + 1].wait()

    b_near(0)
    b_own_y(1)
    a_got("ac")
    expand(slot(0, 1, 0))
    a_got("ax+")
    a_send("af+", slot(0, 0, 3), right)
    a_send("c3", slot(0, 0, 3), sib)
    a_got("ax-")
    a_send("af-", slot(0, 0, 1), left)
    a_send("c1", slot(0, 0, 1), sib)
    expand(slot(0, 0, 3))
    expand(slot(0, 0, 1))
    b_partner(0)
    b_own_z(1)
    a_got("az")
    a_send("bx+", slot(1, 0, 0), right)
    a_send("bx-", slot(1, 0, 0), left)
    a_send("bc", slot(1, 0, 0), sib)
    b_near(1)
    a_got("af+", "af-")
    a_send("c2", slot(0, 0, 2), sib)
    expand(slot(1, 0, 0))
    expand(slot(0, 0, 2))
    for n in ("c1", "c3", "c2"):
        a_got(n)
        expand(A_LANDS[n][0])
    b_far(0)
    b_partner(1)
    a_got("bx+")
    a_send("bf+", slot(1, 0, 3), right)
    a_send("d3", slot(1, 0, 3), sib)
    a_got("bx-")
    a_send("bf-", slot(1, 0, 1), left)
    a_send("d1", slot(1, 0, 1), sib)
    expand(slot(1, 0, 3))
    expand(slot(1, 0, 1))
    a_got("bc")
    expand(slot(1, 1, 0))
    b_got(0, "fp", "fm", "zhp", "zhm", "gp", "gm")
    pl.loop(0, 4)(left_part)
    b_far(1)
    pl.loop(4, 8)(left_part)
    a_got("bf+", "bf-")
    a_send("d2", slot(1, 0, 2), sib)
    expand(slot(1, 0, 2))
    for n in ("d1", "d3", "d2"):
        a_got(n)
        expand(A_LANDS[n][0])
    pl.loop(8, 16)(left_part)
    left_out = pltpu.make_async_copy(acc0, out.at[:, pl.ds(0, H)], ls.at[0])
    left_out.start()
    b_got(1, "fp", "fm")
    pl.loop(0, 5)(right_part)
    b_got(1, "zhp", "zhm")
    right_part(jnp.int32(5))
    right_part(jnp.int32(7))
    b_got(1, "gp", "gm")
    right_part(jnp.int32(6))
    right_out = pltpu.make_async_copy(acc1, out.at[:, pl.ds(H, H)], ls.at[1])
    right_out.start()
    for c in started:
        c.wait_send()
    left_out.wait()
    right_out.wait()


def local_step(amplitudes, integrals, screen_mask, tile_order):
    n = len(IDS)
    scratch = [pltpu.VMEM((CAP + 1, T, T), jnp.bfloat16)] * 16 + [pltpu.SMEM((64,), jnp.int32)] * 16
    scratch += [
        pltpu.VMEM((KT * ROWT, T, T), jnp.bfloat16),
        pltpu.VMEM((64, M, T), jnp.bfloat16),
        pltpu.VMEM((8 * DEPTH, T, H), jnp.bfloat16),
        pltpu.VMEM((8 * DEPTH, T, H), jnp.bfloat16),
        pltpu.VMEM((M, H), jnp.float32),
        pltpu.VMEM((M, H), jnp.float32),
        pltpu.VMEM((8, 128), jnp.int32),
        pltpu.SMEM((8, 128), jnp.int32),
        pltpu.SMEM((KT * ROWT + 2,), jnp.int32),
        pltpu.SMEM((KT * ROWT + 2,), jnp.int32),
        pltpu.SMEM((KT * ROWT + 2,), jnp.int32),
        pltpu.SemaphoreType.DMA((n,)),
        pltpu.SemaphoreType.DMA((n,)),
        pltpu.SemaphoreType.DMA((KT + 3,)),
    ]
    anywhere = pl.BlockSpec(memory_space=pl.ANY)
    scalars = pl.BlockSpec(memory_space=pltpu.SMEM)
    return pl.pallas_call(
        kernel,
        out_shape=jax.ShapeDtypeStruct((M, 2 * H), jnp.float32),
        in_specs=[anywhere, anywhere, scalars, scalars],
        out_specs=anywhere,
        scratch_shapes=scratch,
        cost_estimate=pl.CostEstimate(flops=2 * M * 512 * 8192, bytes_accessed=6 << 20, transcendentals=0),
        compiler_params=pltpu.CompilerParams(
            collective_id=0, has_side_effects=True, vmem_limit_bytes=58 << 20
        ),
    )(amplitudes.reshape(ROWT, T, KT * T), integrals.reshape(DEPTH, T, 2 * H), screen_mask, tile_order)


def solution(mesh):
    placed = (P("row", "col"), P("row", "col"), P("row", "col"), P())
    return jax.shard_map(
        local_step, mesh=mesh, in_specs=placed, out_specs=P("row", "col"), check_vma=False
    )
```

```python
import jax
import jax.numpy as jnp
from jax import lax
from jax.experimental import pallas as pl
from jax.experimental.pallas import tpu as pltpu
from jax.sharding import PartitionSpec as P

MESH = pl.DeviceIdType.MESH
T = 128
ROWT, KT, CAP = 12, 4, 24
M = ROWT * T
DEPTH = 8
H = 256
ZERO = CAP
CUT = 5
CHUNK = 768

B_IDS = ("zp", "yp", "ym", "pp", "pm", "fp", "fm", "zhp", "zhm", "gp", "gm")
A_IDS = ("ax+", "ax-", "az", "ac", "bx+", "bx-", "bc", "af+", "af-", "bf+", "bf-",
         "c1", "c2", "c3", "d1", "d2", "d3")
IDS = {}
for _h in (0, 1):
    for _n in B_IDS:
        IDS[(_n, _h)] = len(IDS)
for _n in A_IDS:
    IDS[_n] = len(IDS)
for _n in A_IDS:
    if _n not in ("af-", "bf-"):
        IDS[("m", _n)] = len(IDS)


def kernel(a_in, b_in, mask, order, out, *scratch):
    A = scratch[0:16]
    meta = scratch[16:32]
    (a_loc, dense, b0, b1, inv_v, inv_s, nxt, pos, cnt, ss, rs, ls) = scratch[32:]
    B = (b0, b1)
    row, col = lax.axis_index("row"), lax.axis_index("col")
    y, zl = lax.rem(row, 4), lax.div(row, 4)
    core, zh, x = lax.rem(col, 2), lax.rem(lax.div(col, 2), 2), lax.div(col, 4)

    def at(dx=0, dy=0, dzl=0, dzh=0, dcore=0):
        r = lax.rem(zl + dzl, 2) * 4 + lax.rem(y + dy, 4)
        c = (lax.rem(x + dx, 4) * 2 + lax.rem(zh + dzh, 2)) * 2 + lax.rem(core + dcore, 2)
        return r, c

    up, down, zpart = at(dy=1), at(dy=3), at(dzl=1)
    right, left, hpart, sib = at(dx=1), at(dx=3), at(dzh=1), at(dcore=1)
    peers = (up, down, zpart, right, left, hpart, sib)

    barrier = pltpu.get_barrier_semaphore()
    for p in peers:
        pl.semaphore_signal(barrier, inc=1, device_id=p, device_id_type=MESH)

    local = []
    for k in range(KT):
        local.append(pltpu.make_async_copy(a_in.at[:, :, pl.ds(k * T, T)], a_loc.at[pl.ds(k * ROWT, ROWT)], ls.at[k]))
    for h in (0, 1):
        local.append(pltpu.make_async_copy(b_in.at[:, :, pl.ds(h * H, H)], B[h].at[pl.ds(row * DEPTH, DEPTH)], ls.at[KT + h]))
    for c in local:
        c.start()
    pl.semaphore_wait(barrier, len(peers))

    started = []

    def send(name, src, dst, device):
        i = IDS[name]
        c = pltpu.make_async_remote_copy(src, dst, ss.at[i], rs.at[i], device_id=device, device_id_type=MESH)
        c.start()
        started.append(c)

    def got(name, ref):
        i = IDS[name]
        pltpu.make_async_remote_copy(ref, ref, ss.at[i], rs.at[i], device_id=sib, device_id_type=MESH).wait_recv()

    def rows_of(h, dzl, dy, first=0, count=DEPTH):
        r = lax.rem(zl + dzl, 2) * 4 + lax.rem(y + dy, 4)
        return B[h].at[pl.ds(r * DEPTH + first, count)]

    def b_send(name, h, dzl, dy, device, first=0, count=DEPTH, own=False):
        dst = rows_of(h, dzl, dy, first, count)
        src = b_in.at[:, :, pl.ds(h * H, H)] if own else dst
        send((name, h), src, dst, device)

    HALF = DEPTH // 2
    LANDS = {
        "zp": (1, 0, 0, DEPTH), "yp": (0, 3, 0, DEPTH), "ym": (0, 1, 0, DEPTH),
        "pp": (1, 3, 0, CUT), "pm": (1, 1, DEPTH - CUT, CUT),
        "fp": (0, 2, 0, HALF), "fm": (0, 2, HALF, HALF),
        "zhp": (1, 3, CUT, DEPTH - CUT), "zhm": (1, 1, 0, DEPTH - CUT),
        "gp": (1, 2, 0, HALF), "gm": (1, 2, HALF, HALF),
    }

    def b_got(h, *names):
        for n in names:
            got((n, h), rows_of(h, *LANDS[n]))

    def b_own_y(h):
        b_send("yp", h, 0, 0, up, own=True)
        b_send("ym", h, 0, 0, down, own=True)

    def b_own_z(h):
        b_send("zp", h, 0, 0, zpart, own=True)

    def b_near(h):
        b_got(h, "yp")
        b_send("fp", h, 0, 3, up, 0, HALF)
        b_got(h, "ym")
        b_send("fm", h, 0, 1, down, HALF, HALF)
        b_send("zhp", h, 0, 3, zpart, CUT, DEPTH - CUT)
        b_send("zhm", h, 0, 1, zpart, 0, DEPTH - CUT)

    def b_partner(h):
        b_got(h, "zp")
        b_send("pp", h, 1, 0, up, 0, CUT)
        b_send("pm", h, 1, 0, down, DEPTH - CUT, CUT)

    def b_far(h):
        b_got(h, "pp")
        b_send("gp", h, 1, 3, up, 0, HALF)
        b_got(h, "pm")
        b_send("gm", h, 1, 1, down, HALF, HALF)

    def slot(dzh, dcore, dx):
        return dzh * 8 + dcore * 4 + dx

    A_LANDS = {
        "ax+": (slot(0, 0, 3), 0, CAP), "ax-": (slot(0, 0, 1), 0, CAP),
        "az": (slot(1, 0, 0), 0, CAP), "ac": (slot(0, 1, 0), 0, CAP),
        "bx+": (slot(1, 0, 3), 0, CAP), "bx-": (slot(1, 0, 1), 0, CAP), "bc": (slot(1, 1, 0), 0, CAP),
        "af+": (slot(0, 0, 2), 0, CAP // 2), "af-": (slot(0, 0, 2), CAP // 2, CAP // 2),
        "bf+": (slot(1, 0, 2), 0, CAP // 2), "bf-": (slot(1, 0, 2), CAP // 2, CAP // 2),
        "c1": (slot(0, 1, 1), 0, CAP), "c2": (slot(0, 1, 2), 0, CAP), "c3": (slot(0, 1, 3), 0, CAP),
        "d1": (slot(1, 1, 1), 0, CAP), "d2": (slot(1, 1, 2), 0, CAP), "d3": (slot(1, 1, 3), 0, CAP),
    }

    def a_send(name, src, device):
        s, first, count = A_LANDS[name]
        rows = pl.ds(first, count)
        send(name, A[src].at[rows], A[s].at[rows], device)
        if ("m", name) in IDS:
            send(("m", name), meta[src], meta[s], device)

    def a_got(*names):
        for n in names:
            s, first, count = A_LANDS[n]
            got(n, A[s].at[pl.ds(first, count)])
            if ("m", n) in IDS:
                got(("m", n), meta[s])

    def col_of(g):
        dzh, dcore, dx = lax.div(g, 8), lax.rem(lax.div(g, 4), 2), lax.rem(g, 4)
        return (lax.rem(x + dx, 4) * 2 + lax.rem(zh + dzh, 2)) * 2 + lax.rem(core + dcore, 2)

    def expand(s):
        base = col_of(jnp.int32(s)) * KT

        @pl.loop(0, KT * ROWT)
        def _(t):
            rows = pl.ds(pl.multiple_of(lax.rem(t, ROWT) * T, T), T)
            dense[base + lax.div(t, ROWT), rows, :] = A[s][meta[s][t]]

    def left_part(g):
        c = col_of(g)
        for m in range(M // CHUNK):
            lhs = jnp.concatenate(
                [dense[c * KT + j, pl.ds(m * CHUNK, CHUNK), :] for j in range(KT)], axis=1)
            rhs = jnp.concatenate(
                [b0[order[c * KT + j]] for j in range(KT)], axis=0)
            out[pl.ds(m * CHUNK, CHUNK), pl.ds(0, H)] += jnp.dot(lhs, rhs, preferred_element_type=jnp.float32)

    def right_part(g):
        r = lax.rem(zl + lax.div(g, 4), 2) * 4 + lax.rem(y + lax.rem(g, 4), 4)
        for m in range(M // CHUNK):
            for q in (0, 1):
                lhs = jnp.concatenate(
                    [dense[inv_s[0, r * 8 + q * 4 + j], pl.ds(m * CHUNK, CHUNK), :]
                     for j in range(4)], axis=1)
                rhs = b1[pl.ds(r * DEPTH + q * 4, 4)].reshape(4 * T, H)
                out[pl.ds(m * CHUNK, CHUNK), pl.ds(H, H)] += jnp.dot(lhs, rhs, preferred_element_type=jnp.float32)

    b_own_y(0)
    b_own_z(0)

    nxt[KT * ROWT] = 0

    @pl.loop(0, KT * ROWT)
    def _(n):
        t = KT * ROWT - 1 - n
        keep = mask[lax.div(t, ROWT), lax.rem(t, ROWT)]
        nxt[t] = keep * t + (1 - keep) * nxt[t + 1]

    cnt[0] = 0

    @pl.loop(0, KT * ROWT)
    def _(t):
        keep = mask[lax.div(t, ROWT), lax.rem(t, ROWT)]
        meta[0][t] = keep * cnt[t] + (1 - keep) * ZERO
        cnt[t + 1] = cnt[t] + keep

    for k in range(KT):
        local[k].wait()
    pos[0] = nxt[0]

    @pl.loop(0, CAP)
    def _(s):
        A[0][s] = a_loc[pos[s]]
        pos[s + 1] = nxt[pos[s] + 1]

    a_send("ax+", 0, right)
    a_send("ax-", 0, left)
    a_send("az", 0, hpart)
    a_send("ac", 0, sib)

    lane = lax.broadcasted_iota(jnp.int32, (8, 128), 1)
    inv_v[...] = jnp.zeros((8, 128), jnp.int32)

    @pl.loop(0, 64)
    def _(k):
        apart = lane - order[k]
        inv_v[...] += (k - inv_v[...]) * (1 - jnp.minimum(jnp.maximum(apart, -apart), 1))

    to_s = pltpu.make_async_copy(inv_v, inv_s, ls.at[KT + 2])
    to_s.start()
    for s in range(16):
        A[s][ZERO] = jnp.zeros((T, T), jnp.bfloat16)
    out[...] = jnp.zeros_like(out)
    expand(0)
    to_s.wait()
    local[KT].wait()
    local[KT + 1].wait()

    b_near(0)
    b_own_y(1)
    a_got("ac")
    expand(slot(0, 1, 0))
    a_got("ax+")
    a_send("af+", slot(0, 0, 3), right)
    a_send("c3", slot(0, 0, 3), sib)
    a_got("ax-")
    a_send("af-", slot(0, 0, 1), left)
    a_send("c1", slot(0, 0, 1), sib)
    expand(slot(0, 0, 3))
    expand(slot(0, 0, 1))
    b_partner(0)
    b_own_z(1)
    a_got("az")
    a_send("bx+", slot(1, 0, 0), right)
    a_send("bx-", slot(1, 0, 0), left)
    a_send("bc", slot(1, 0, 0), sib)
    b_near(1)
    a_got("af+", "af-")
    a_send("c2", slot(0, 0, 2), sib)
    expand(slot(1, 0, 0))
    expand(slot(0, 0, 2))
    for n in ("c1", "c3", "c2"):
        a_got(n)
        expand(A_LANDS[n][0])
    b_far(0)
    b_partner(1)
    a_got("bx+")
    a_send("bf+", slot(1, 0, 3), right)
    a_send("d3", slot(1, 0, 3), sib)
    a_got("bx-")
    a_send("bf-", slot(1, 0, 1), left)
    a_send("d1", slot(1, 0, 1), sib)
    expand(slot(1, 0, 3))
    expand(slot(1, 0, 1))
    a_got("bc")
    expand(slot(1, 1, 0))
    b_got(0, "fp", "fm", "zhp", "zhm", "gp", "gm")
    pl.loop(0, 4)(left_part)
    b_far(1)
    pl.loop(4, 8)(left_part)
    a_got("bf+", "bf-")
    a_send("d2", slot(1, 0, 2), sib)
    expand(slot(1, 0, 2))
    for n in ("d1", "d3", "d2"):
        a_got(n)
        expand(A_LANDS[n][0])
    pl.loop(8, 16)(left_part)
    b_got(1, "fp", "fm")
    pl.loop(0, 5)(right_part)
    b_got(1, "zhp", "zhm")
    right_part(jnp.int32(5))
    right_part(jnp.int32(7))
    b_got(1, "gp", "gm")
    right_part(jnp.int32(6))
    for c in started:
        c.wait_send()


def local_step(amplitudes, integrals, screen_mask, tile_order):
    n = len(IDS)
    scratch = [pltpu.VMEM((CAP + 1, T, T), jnp.bfloat16)] * 16 + [pltpu.SMEM((64,), jnp.int32)] * 16
    scratch += [
        pltpu.VMEM((KT * ROWT, T, T), jnp.bfloat16),
        pltpu.VMEM((64, M, T), jnp.bfloat16),
        pltpu.VMEM((8 * DEPTH, T, H), jnp.bfloat16),
        pltpu.VMEM((8 * DEPTH, T, H), jnp.bfloat16),
        pltpu.VMEM((8, 128), jnp.int32),
        pltpu.SMEM((8, 128), jnp.int32),
        pltpu.SMEM((KT * ROWT + 2,), jnp.int32),
        pltpu.SMEM((KT * ROWT + 2,), jnp.int32),
        pltpu.SMEM((KT * ROWT + 2,), jnp.int32),
        pltpu.SemaphoreType.DMA((n,)),
        pltpu.SemaphoreType.DMA((n,)),
        pltpu.SemaphoreType.DMA((KT + 3,)),
    ]
    anywhere = pl.BlockSpec(memory_space=pl.ANY)
    scalars = pl.BlockSpec(memory_space=pltpu.SMEM)
    return pl.pallas_call(
        kernel,
        out_shape=pltpu.VMEM((M, 2 * H), jnp.float32),
        in_specs=[anywhere, anywhere, scalars, scalars],
        out_specs=pl.BlockSpec(memory_space=pltpu.VMEM),
        scratch_shapes=scratch,
        cost_estimate=pl.CostEstimate(flops=2 * M * 512 * 8192, bytes_accessed=6 << 20, transcendentals=0),
        compiler_params=pltpu.CompilerParams(
            collective_id=0, has_side_effects=True, vmem_limit_bytes=58 << 20
        ),
    )(amplitudes.reshape(ROWT, T, KT * T), integrals.reshape(DEPTH, T, 2 * H), screen_mask.T, tile_order)


def solution(mesh):
    placed = (P("row", "col"), P("row", "col"), P("row", "col"), P())
    return jax.shard_map(
        local_step, mesh=mesh, in_specs=placed, out_specs=P("row", "col"), check_vma=False
    )
```

```python
import jax
import jax.numpy as jnp
from jax import lax
from jax.experimental import pallas as pl
from jax.experimental.pallas import tpu as pltpu
from jax.sharding import PartitionSpec as P

MESH = pl.DeviceIdType.MESH
T = 128
ROWT, KT, CAP = 12, 4, 24
M = ROWT * T
DEPTH = 8
H = 256
ZERO = CAP
CHUNK = 768

TRANSFERS = {
    "0U1": ("u", (0, 3), 0, 4),
    "0U2": ("u", (0, 3), 4, 4),
    "0D1": ("d", (0, 1), 4, 4),
    "0D2": ("d", (0, 1), 0, 4),
    "0Z1": ("z", (1, 0), 0, 4),
    "0Z2": ("z", (1, 0), 4, 4),
    "0FU": ("u", (0, 2), 0, 4),
    "0FD": ("d", (0, 2), 4, 4),
    "0PU1": ("u", (1, 3), 0, 4),
    "0PD1": ("d", (1, 1), 4, 4),
    "0PU2": ("u", (1, 3), 4, 2),
    "0PD2": ("d", (1, 1), 2, 2),
    "0ZU": ("z", (1, 3), 6, 2),
    "0ZD": ("z", (1, 1), 0, 2),
    "0GU": ("u", (1, 2), 0, 4),
    "0GD": ("d", (1, 2), 4, 4),
    "XR1": ("r", (0, 0, 3), 0, 12),
    "XR2": ("r", (0, 0, 3), 12, 12),
    "XL1": ("l", (0, 0, 1), 12, 12),
    "XL2": ("l", (0, 0, 1), 0, 12),
    "XFR": ("r", (0, 0, 2), 0, 12),
    "XFL": ("l", (0, 0, 2), 12, 12),
    "XS0": ("s", (0, 1, 0), 0, 24),
    "XS3": ("s", (0, 1, 3), 0, 24),
    "XS1": ("s", (0, 1, 1), 0, 24),
    "XT2": ("s", (0, 1, 2), 0, 12),
    "XU2": ("s", (0, 1, 2), 12, 12),
    "YR1": ("r", (1, 0, 3), 0, 12),
    "YR2": ("r", (1, 0, 3), 12, 12),
    "YL1": ("l", (1, 0, 1), 12, 12),
    "YL2": ("l", (1, 0, 1), 0, 12),
    "YFR": ("r", (1, 0, 2), 0, 12),
    "YFL": ("l", (1, 0, 2), 12, 12),
    "YS0": ("s", (1, 1, 0), 0, 24),
    "YS3": ("s", (1, 1, 3), 0, 24),
    "YS1": ("s", (1, 1, 1), 0, 24),
    "YT2": ("s", (1, 1, 2), 0, 12),
    "YU2": ("s", (1, 1, 2), 12, 12),
    "H1": ("z", (1, 0, 0), 0, 12),
    "H2": ("z", (1, 0, 0), 12, 12),
    "1U1": ("u", (0, 3), 0, 4),
    "1U2": ("u", (0, 3), 4, 4),
    "1D1": ("d", (0, 1), 4, 4),
    "1D2": ("d", (0, 1), 0, 4),
    "1Z1": ("z", (1, 0), 0, 4),
    "1Z2": ("z", (1, 0), 4, 4),
    "1FU": ("u", (0, 2), 0, 4),
    "1FD": ("d", (0, 2), 4, 4),
    "1PU1": ("u", (1, 3), 0, 4),
    "1PD1": ("d", (1, 1), 4, 4),
    "1PU2": ("u", (1, 3), 4, 2),
    "1PD2": ("d", (1, 1), 2, 2),
    "1ZU": ("z", (1, 3), 6, 2),
    "1ZD": ("z", (1, 1), 0, 2),
    "1GU": ("u", (1, 2), 0, 4),
    "1GD": ("d", (1, 2), 4, 4),
}
ORDER = [
    "S 0Z2", "S 0D1", "prep", "S XR2", "S XL2", "S 0U2", "S 1D2", "S H1", "S 0U1", "S XS0", "S H2", "W 0D1", "S XR1",
    "S XL1", "W 0Z2", "S 0PD1", "S 0FD", "W XR2", "S 1U1", "W H1", "S 0Z1", "W XL2", "S YL2", "S YR1", "S 1Z1",
    "W 0U1", "S 0FU", "S 0D2", "W XL1", "S XS1", "S 1U2", "W 1U1", "W H2", "W 0PD1", "S YL1", "prep2", "W 0U2",
    "S 1D1", "S 1Z2", "W XR1", "S YR2", "W YL2", "W 0Z1", "S 0PU1", "S 0PD2", "S 0GD", "S YS0", "S XS3", "S XFR",
    "S 0PU2", "W XS0", "W 1U2", "W 0D2", "S XFL", "S 0ZU", "W YR1", "W 1D2", "W YL1", "S YS1", "E 9", "W 1D1",
    "W 0PU1", "S 0GU", "W 0FD", "E 1", "W YR2", "S YS3", "W 1Z1", "S 0ZD", "W YS1", "S 1PD2", "W 0PU2", "E 13",
    "S 1PU1", "W XS3", "W 0PD2", "W 1Z2", "W YS3", "W XS1", "S YFR", "E 7", "E 5", "W 0FU", "E 11", "S 1PD1", "E 15",
    "S 1ZD", "S 1PU2", "E 0", "S YFL", "E 3", "W 0ZU", "W YS0", "S 1ZU", "W 0GD", "E 4", "E 8", "E 12", "S 1FU",
    "S 1FD", "W XFR", "S XT2", "W XFL", "E 2", "S XU2", "W 0GU", "W 1PD2", "W 0ZD", "P 4 3", "P 13 0", "P 2 11",
    "W XT2", "P 1 8", "P 9 7", "P 12 15", "W XU2", "E 6", "W 1PU1", "W 1PD1", "S 1GU", "W YFR", "S YT2", "S 1GD",
    "W YFL", "W 1ZU", "S YU2", "L 5", "E 10", "W 1PU2", "W YT2", "W 1ZD", "L 10", "W YU2", "E 14", "R 4", "R 1",
    "L 14", "W 1FD", "R 7", "R 3", "R 0", "R 5", "L 6", "W 1FU", "W 1GD", "Q 1", "R 2", "W 1GU", "Q 0",
]
IDS = {}
for _n, _t in TRANSFERS.items():
    IDS[_n] = len(IDS)
    if len(_t[1]) == 3 and _t[2] == 0:
        IDS["m" + _n] = len(IDS)


def kernel(a_in, b_in, mask, order, out, *scratch):
    A = scratch[0:16]
    meta = scratch[16:32]
    (a_loc, dense, b0, b1, inv_v, inv_s, nxt, pos, cnt, ss, rs, ls) = scratch[32:]
    B = (b0, b1)
    row, col = lax.axis_index("row"), lax.axis_index("col")
    y, zl = lax.rem(row, 4), lax.div(row, 4)
    core, zh, x = lax.rem(col, 2), lax.rem(lax.div(col, 2), 2), lax.div(col, 4)

    def at(dx=0, dy=0, dzl=0, dzh=0, dcore=0):
        r = lax.rem(zl + dzl, 2) * 4 + lax.rem(y + dy, 4)
        c = (lax.rem(x + dx, 4) * 2 + lax.rem(zh + dzh, 2)) * 2 + lax.rem(core + dcore, 2)
        return r, c

    up, down, zpart = at(dy=1), at(dy=3), at(dzl=1)
    right, left, hpart, sib = at(dx=1), at(dx=3), at(dzh=1), at(dcore=1)
    peers = (up, down, zpart, right, left, hpart, sib)

    barrier = pltpu.get_barrier_semaphore()
    for p in peers:
        pl.semaphore_signal(barrier, inc=1, device_id=p, device_id_type=MESH)

    local = []
    for k in range(KT):
        local.append(pltpu.make_async_copy(a_in.at[:, :, pl.ds(k * T, T)], a_loc.at[pl.ds(k * ROWT, ROWT)], ls.at[k]))
    for h in (0, 1):
        local.append(pltpu.make_async_copy(b_in.at[:, :, pl.ds(h * H, H)], B[h].at[pl.ds(row * DEPTH, DEPTH)], ls.at[KT + h]))
    for c in local:
        c.start()
    pl.semaphore_wait(barrier, len(peers))

    started = []

    def start(i, src, dst, device):
        c = pltpu.make_async_remote_copy(src, dst, ss.at[i], rs.at[i], device_id=device, device_id_type=MESH)
        c.start()
        started.append(c)

    def arrived(i, ref):
        pltpu.make_async_remote_copy(ref, ref, ss.at[i], rs.at[i], device_id=sib, device_id_type=MESH).wait_recv()

    def slot(dzh, dcore, dx):
        return dzh * 8 + dcore * 4 + dx

    def block(h, dzl, dy, first, count):
        r = lax.rem(zl + dzl, 2) * 4 + lax.rem(y + dy, 4)
        return B[h].at[pl.ds(r * DEPTH + first, count)]

    def send(name):
        way, land, first, count = TRANSFERS[name]
        if len(land) == 2:
            h, (dzl, dy) = int(name[0]), land
            dzl, dy = {"u": (dzl, dy + 1), "d": (dzl, dy + 3), "z": (1 - dzl, dy)}[way]
            dst = block(h, dzl, dy % 4, first, count)
            src = b_in.at[pl.ds(first, count), :, pl.ds(h * H, H)] if (dzl, dy % 4) == (0, 0) else dst
            start(IDS[name], src, dst, {"u": up, "d": down, "z": zpart}[way])
        else:
            dzh, dcore, dx = land
            frm = {"r": (dzh, dcore, dx + 1), "l": (dzh, dcore, dx + 3),
                   "z": (1 - dzh, dcore, dx), "s": (dzh, 1 - dcore, dx)}[way]
            frm, to = slot(frm[0], frm[1], frm[2] % 4), slot(*land)
            device = {"r": right, "l": left, "z": hpart, "s": sib}[way]
            tiles = pl.ds(first, count)
            start(IDS[name], A[frm].at[tiles], A[to].at[tiles], device)
            if first == 0:
                start(IDS["m" + name], meta[frm], meta[to], device)

    def wait(name):
        _, land, first, count = TRANSFERS[name]
        if len(land) == 2:
            arrived(IDS[name], block(int(name[0]), *land, first, count))
        else:
            s = slot(*land)
            arrived(IDS[name], A[s].at[pl.ds(first, count)])
            if first == 0:
                arrived(IDS["m" + name], meta[s])

    def col_of(s):
        dzh, dcore, dx = s // 8, s // 4 % 2, s % 4
        return at(dx=dx, dzh=dzh, dcore=dcore)[1]

    def expand(s):
        base = col_of(s) * KT

        @pl.loop(0, KT)
        def _(j):
            for i in range(ROWT):
                dense[base + j, pl.ds(i * T, T), :] = A[s][meta[s][j * ROWT + i]]

    def add(half, left_tiles, right_tiles):
        rhs = jnp.concatenate(right_tiles, axis=0)
        for m in range(M // CHUNK):
            rows = pl.ds(m * CHUNK, CHUNK)
            lhs = jnp.concatenate([dense[k, rows, :] for k in left_tiles], axis=1)
            out[rows, pl.ds(half * H, H)] += jnp.dot(lhs, rhs, preferred_element_type=jnp.float32)

    def left_part(*slots):
        tiles = [col_of(s) * KT + j for s in slots for j in range(KT)]
        add(0, tiles, [b0[order[k]] for k in tiles])

    def right_part(g, first=0, count=DEPTH):
        r = at(dzl=g // 4, dy=g % 4)[0]
        tiles = [r * DEPTH + first + j for j in range(count)]
        add(1, [inv_s[0, t] for t in tiles], [b1[t] for t in tiles])

    def prepare():
        nxt[KT * ROWT] = 0

        @pl.loop(0, KT * ROWT)
        def _(n):
            t = KT * ROWT - 1 - n
            keep = mask[lax.div(t, ROWT), lax.rem(t, ROWT)]
            nxt[t] = keep * t + (1 - keep) * nxt[t + 1]

        cnt[0] = 0

        @pl.loop(0, KT * ROWT)
        def _(t):
            keep = mask[lax.div(t, ROWT), lax.rem(t, ROWT)]
            meta[0][t] = keep * cnt[t] + (1 - keep) * ZERO
            cnt[t + 1] = cnt[t] + keep

        for k in range(KT):
            local[k].wait()
        pos[0] = nxt[0]

        @pl.loop(0, CAP)
        def _(s):
            A[0][s] = a_loc[pos[s]]
            pos[s + 1] = nxt[pos[s] + 1]

    def prepare_rest():
        lane = lax.broadcasted_iota(jnp.int32, (8, 128), 1)
        inv_v[...] = jnp.zeros((8, 128), jnp.int32)

        @pl.loop(0, 64)
        def _(k):
            apart = lane - order[k]
            inv_v[...] += (k - inv_v[...]) * (1 - jnp.minimum(jnp.maximum(apart, -apart), 1))

        to_s = pltpu.make_async_copy(inv_v, inv_s, ls.at[KT + 2])
        to_s.start()
        for s in range(16):
            A[s][ZERO] = jnp.zeros((T, T), jnp.bfloat16)
        out[...] = jnp.zeros_like(out)
        to_s.wait()
        local[KT].wait()
        local[KT + 1].wait()

    for step in ORDER:
        what, *which = step.split()
        if what == "S":
            send(which[0])
        elif what == "W":
            wait(which[0])
        elif what == "E":
            expand(int(which[0]))
        elif what == "prep":
            prepare()
        elif what == "prep2":
            prepare_rest()
        elif what in "LP":
            left_part(*map(int, which))
        elif what == "R":
            right_part(int(which[0]))
        else:
            right_part(6, int(which[0]) * 4, 4)
    for c in started:
        c.wait_send()


def local_step(amplitudes, integrals, screen_mask, tile_order):
    n = len(IDS)
    scratch = [pltpu.VMEM((CAP + 1, T, T), jnp.bfloat16)] * 16 + [pltpu.SMEM((64,), jnp.int32)] * 16
    scratch += [
        pltpu.VMEM((KT * ROWT, T, T), jnp.bfloat16),
        pltpu.VMEM((64, M, T), jnp.bfloat16),
        pltpu.VMEM((8 * DEPTH, T, H), jnp.bfloat16),
        pltpu.VMEM((8 * DEPTH, T, H), jnp.bfloat16),
        pltpu.VMEM((8, 128), jnp.int32),
        pltpu.SMEM((8, 128), jnp.int32),
        pltpu.SMEM((KT * ROWT + 2,), jnp.int32),
        pltpu.SMEM((KT * ROWT + 2,), jnp.int32),
        pltpu.SMEM((KT * ROWT + 2,), jnp.int32),
        pltpu.SemaphoreType.DMA((n,)),
        pltpu.SemaphoreType.DMA((n,)),
        pltpu.SemaphoreType.DMA((KT + 3,)),
    ]
    anywhere = pl.BlockSpec(memory_space=pl.ANY)
    scalars = pl.BlockSpec(memory_space=pltpu.SMEM)
    return pl.pallas_call(
        kernel,
        out_shape=pltpu.VMEM((M, 2 * H), jnp.float32),
        in_specs=[anywhere, anywhere, scalars, scalars],
        out_specs=pl.BlockSpec(memory_space=pltpu.VMEM),
        scratch_shapes=scratch,
        cost_estimate=pl.CostEstimate(flops=2 * M * 512 * 8192, bytes_accessed=6 << 20, transcendentals=0),
        compiler_params=pltpu.CompilerParams(
            collective_id=0, has_side_effects=True, vmem_limit_bytes=58 << 20
        ),
    )(amplitudes.reshape(ROWT, T, KT * T), integrals.reshape(DEPTH, T, 2 * H), screen_mask.T, tile_order)


def solution(mesh):
    placed = (P("row", "col"), P("row", "col"), P("row", "col"), P())
    return jax.shard_map(
        local_step, mesh=mesh, in_specs=placed, out_specs=P("row", "col"), check_vma=False
    )
```

```python
import jax
import jax.numpy as jnp
from jax import lax
from jax.experimental import pallas as pl
from jax.experimental.pallas import tpu as pltpu
from jax.sharding import PartitionSpec as P

MESH = pl.DeviceIdType.MESH
T = 128
ROWT, KT, CAP = 12, 4, 24
M = ROWT * T
DEPTH = 8
H = 256
ZERO = CAP
CHUNK = 768

TRANSFERS = {
    "0U1": ("u", (0, 3), 0, 4),
    "0U2": ("u", (0, 3), 4, 4),
    "0D1": ("d", (0, 1), 4, 4),
    "0D2": ("d", (0, 1), 0, 4),
    "0Z1": ("z", (1, 0), 0, 4),
    "0Z2": ("z", (1, 0), 4, 4),
    "0FU": ("u", (0, 2), 0, 4),
    "0FD": ("d", (0, 2), 4, 4),
    "0PU1": ("u", (1, 3), 0, 4),
    "0PD1": ("d", (1, 1), 4, 4),
    "0PU2": ("u", (1, 3), 4, 2),
    "0PD2": ("d", (1, 1), 2, 2),
    "0ZU": ("z", (1, 3), 6, 2),
    "0ZD": ("z", (1, 1), 0, 2),
    "0GU": ("u", (1, 2), 0, 4),
    "0GD": ("d", (1, 2), 4, 4),
    "XR1": ("r", (0, 0, 3), 0, 12),
    "XR2": ("r", (0, 0, 3), 12, 12),
    "XL1": ("l", (0, 0, 1), 12, 12),
    "XL2": ("l", (0, 0, 1), 0, 12),
    "XFR": ("r", (0, 0, 2), 0, 12),
    "XFL": ("l", (0, 0, 2), 12, 12),
    "XS0": ("s", (0, 1, 0), 0, 24),
    "XS3": ("s", (0, 1, 3), 0, 24),
    "XS1": ("s", (0, 1, 1), 0, 24),
    "XT2": ("s", (0, 1, 2), 0, 12),
    "XU2": ("s", (0, 1, 2), 12, 12),
    "YR1": ("r", (1, 0, 3), 0, 12),
    "YR2": ("r", (1, 0, 3), 12, 12),
    "YL1": ("l", (1, 0, 1), 12, 12),
    "YL2": ("l", (1, 0, 1), 0, 12),
    "YFR": ("r", (1, 0, 2), 0, 12),
    "YFL": ("l", (1, 0, 2), 12, 12),
    "YS0": ("s", (1, 1, 0), 0, 24),
    "YS3": ("s", (1, 1, 3), 0, 24),
    "YS1": ("s", (1, 1, 1), 0, 24),
    "YT2": ("s", (1, 1, 2), 0, 12),
    "YU2": ("s", (1, 1, 2), 12, 12),
    "H1": ("z", (1, 0, 0), 0, 12),
    "H2": ("z", (1, 0, 0), 12, 12),
    "1U1": ("u", (0, 3), 0, 4),
    "1U2": ("u", (0, 3), 4, 4),
    "1D1": ("d", (0, 1), 4, 4),
    "1D2": ("d", (0, 1), 0, 4),
    "1Z1": ("z", (1, 0), 0, 4),
    "1Z2": ("z", (1, 0), 4, 4),
    "1FU": ("u", (0, 2), 0, 4),
    "1FD": ("d", (0, 2), 4, 4),
    "1PU1": ("u", (1, 3), 0, 4),
    "1PD1": ("d", (1, 1), 4, 4),
    "1PU2": ("u", (1, 3), 4, 1),
    "1PD2": ("d", (1, 1), 3, 1),
    "1ZU": ("z", (1, 3), 5, 3),
    "1ZD": ("z", (1, 1), 0, 3),
    "1GU": ("u", (1, 2), 0, 4),
    "1GD": ("d", (1, 2), 4, 4),
}
ORDER = [
    "S 0Z2", "S 0U1", "S 0D1", "prep", "S XL1", "S XR1", "S 0U2", "S H1", "S 1D2", "S 0D2", "S 1U2", "S H2", "W 0D1",
    "S XR2", "S XL2", "W 0Z2", "S 0PU2", "S 1U1", "S 0PD1", "W H1", "W XL1", "S YR1", "W 0U1", "S 0Z1", "prep2",
    "S YL2", "W XR2", "S XS0", "S 0FD", "W XL2", "W 0PU2", "S 1Z2", "W H2", "S 0FU", "S YL1", "W 0PD1", "S 1D1",
    "W XR1", "S YR2", "S XS3", "S XFL", "W 0U2", "W 0Z1", "S 0PU1", "S XFR", "S YS0", "S 1Z1", "W YR1", "W 0D2",
    "S 0PD2", "W 1D1", "W 1D2", "W 1Z2", "S 1PU2", "W 1U2", "W XS0", "S 0GD", "W YR2", "S XS1", "W YL1", "S YFR",
    "W XS3", "S 0ZD", "W 0PD2", "W 0PU1", "S 0GU", "W YL2", "S 0ZU", "E 0", "S YS3", "S YS1", "W XS1", "S YFL", "E 1",
    "W 1U1", "E 4", "E 9", "E 11", "W 0FD", "S 1ZD", "W YS1", "E 7", "W 1Z1", "S 1PD2", "E 8", "S 1PU1", "S 1ZU",
    "S 1PD1", "E 13", "W YS0", "E 3", "W 0GD", "S 1FD", "E 5", "W 0FU", "W XFL", "S XU2", "W XFR", "S XT2", "E 12",
    "S 1FU", "W 1PU2", "E 2", "W YS3", "W 1PD2", "W 0ZD", "E 15", "W 0GU", "W XT2", "W XU2", "E 6", "W 0ZU",
    "L 3 5 13 15", "L 12 2 11 7", "L 1 4 6 0", "L 9", "W 1PD1", "S 1GD", "W 1PU1", "W 1ZD", "W YFL", "W YFR", "S YU2",
    "S 1GU", "S YT2", "E 10", "L 8 10", "W YU2", "W YT2", "E 14", "R 6 7 10 11", "R 8 9", "W 1ZU", "W 1FU", "W 1FD",
    "R 4 5 0 1", "R 14 15 2 3", "L 14", "W 1GD", "R 13", "W 1GU", "R 12",
]
IDS = {}
for _n, _t in TRANSFERS.items():
    IDS[_n] = len(IDS)
    if len(_t[1]) == 3 and _t[2] == 0:
        IDS["m" + _n] = len(IDS)


def kernel(a_in, b_in, mask, order, out, *scratch):
    A = scratch[0:16]
    meta = scratch[16:32]
    (a_loc, dense, b0, b1, inv_v, inv_s, nxt, pos, cnt, ss, rs, ls) = scratch[32:]
    B = (b0, b1)
    row, col = lax.axis_index("row"), lax.axis_index("col")
    y, zl = lax.rem(row, 4), lax.div(row, 4)
    core, zh, x = lax.rem(col, 2), lax.rem(lax.div(col, 2), 2), lax.div(col, 4)

    def at(dx=0, dy=0, dzl=0, dzh=0, dcore=0):
        r = lax.rem(zl + dzl, 2) * 4 + lax.rem(y + dy, 4)
        c = (lax.rem(x + dx, 4) * 2 + lax.rem(zh + dzh, 2)) * 2 + lax.rem(core + dcore, 2)
        return r, c

    up, down, zpart = at(dy=1), at(dy=3), at(dzl=1)
    right, left, hpart, sib = at(dx=1), at(dx=3), at(dzh=1), at(dcore=1)
    peers = (up, down, zpart, right, left, hpart, sib)

    barrier = pltpu.get_barrier_semaphore()
    for p in peers:
        pl.semaphore_signal(barrier, inc=1, device_id=p, device_id_type=MESH)

    local = []
    for k in range(KT):
        local.append(pltpu.make_async_copy(a_in.at[:, :, pl.ds(k * T, T)], a_loc.at[pl.ds(k * ROWT, ROWT)], ls.at[k]))
    for h in (0, 1):
        local.append(pltpu.make_async_copy(b_in.at[:, :, pl.ds(h * H, H)], B[h].at[pl.ds(row * DEPTH, DEPTH)], ls.at[KT + h]))
    for c in local:
        c.start()
    nxt[KT * ROWT] = 0

    @pl.loop(0, KT * ROWT)
    def _(n):
        t = KT * ROWT - 1 - n
        keep = mask[lax.div(t, ROWT), lax.rem(t, ROWT)]
        nxt[t] = keep * t + (1 - keep) * nxt[t + 1]

    cnt[0] = 0

    @pl.loop(0, KT * ROWT)
    def _(t):
        keep = mask[lax.div(t, ROWT), lax.rem(t, ROWT)]
        meta[0][t] = keep * cnt[t] + (1 - keep) * ZERO
        cnt[t + 1] = cnt[t] + keep

    pl.semaphore_wait(barrier, len(peers))

    started = []

    def start(i, src, dst, device):
        c = pltpu.make_async_remote_copy(src, dst, ss.at[i], rs.at[i], device_id=device, device_id_type=MESH)
        c.start()
        started.append(c)

    def arrived(i, ref):
        pltpu.make_async_remote_copy(ref, ref, ss.at[i], rs.at[i], device_id=sib, device_id_type=MESH).wait_recv()

    def slot(dzh, dcore, dx):
        return dzh * 8 + dcore * 4 + dx

    def block(h, dzl, dy, first, count):
        r = lax.rem(zl + dzl, 2) * 4 + lax.rem(y + dy, 4)
        return B[h].at[pl.ds(r * DEPTH + first, count)]

    def send(name):
        way, land, first, count = TRANSFERS[name]
        if len(land) == 2:
            h, (dzl, dy) = int(name[0]), land
            dzl, dy = {"u": (dzl, dy + 1), "d": (dzl, dy + 3), "z": (1 - dzl, dy)}[way]
            dst = block(h, dzl, dy % 4, first, count)
            src = b_in.at[pl.ds(first, count), :, pl.ds(h * H, H)] if (dzl, dy % 4) == (0, 0) else dst
            start(IDS[name], src, dst, {"u": up, "d": down, "z": zpart}[way])
        else:
            dzh, dcore, dx = land
            frm = {"r": (dzh, dcore, dx + 1), "l": (dzh, dcore, dx + 3),
                   "z": (1 - dzh, dcore, dx), "s": (dzh, 1 - dcore, dx)}[way]
            frm, to = slot(frm[0], frm[1], frm[2] % 4), slot(*land)
            device = {"r": right, "l": left, "z": hpart, "s": sib}[way]
            tiles = pl.ds(first, count)
            start(IDS[name], A[frm].at[tiles], A[to].at[tiles], device)
            if first == 0:
                start(IDS["m" + name], meta[frm], meta[to], device)

    def wait(name):
        _, land, first, count = TRANSFERS[name]
        if len(land) == 2:
            arrived(IDS[name], block(int(name[0]), *land, first, count))
        else:
            s = slot(*land)
            arrived(IDS[name], A[s].at[pl.ds(first, count)])
            if first == 0:
                arrived(IDS["m" + name], meta[s])

    def col_of(s):
        dzh, dcore, dx = s // 8, s // 4 % 2, s % 4
        return at(dx=dx, dzh=dzh, dcore=dcore)[1]

    def expand(s):
        base = col_of(s) * KT

        @pl.loop(0, KT)
        def _(j):
            for i in range(ROWT):
                dense[base + j, pl.ds(i * T, T), :] = A[s][meta[s][j * ROWT + i]]

    def add(half, left_tiles, right_tiles):
        rhs = jnp.concatenate(right_tiles, axis=0)
        for m in range(M // CHUNK):
            rows = pl.ds(m * CHUNK, CHUNK)
            lhs = jnp.concatenate([dense[k, rows, :] for k in left_tiles], axis=1)
            out[rows, pl.ds(half * H, H)] += jnp.dot(lhs, rhs, preferred_element_type=jnp.float32)

    def left_part(*slots):
        tiles = [col_of(s) * KT + j for s in slots for j in range(KT)]
        add(0, tiles, [b0[order[k]] for k in tiles])

    def right_part(*quads):
        tiles = [at(dzl=q // 8, dy=q // 2 % 4)[0] * DEPTH + q % 2 * 4 + j for q in quads for j in range(4)]
        add(1, [inv_s[0, t] for t in tiles], [b1[t] for t in tiles])

    def prepare():
        for k in range(KT):
            local[k].wait()
        pos[0] = nxt[0]

        @pl.loop(0, CAP)
        def _(s):
            A[0][s] = a_loc[pos[s]]
            pos[s + 1] = nxt[pos[s] + 1]

    def prepare_rest():
        lane = lax.broadcasted_iota(jnp.int32, (8, 128), 1)
        inv_v[...] = jnp.zeros((8, 128), jnp.int32)

        @pl.loop(0, 64)
        def _(k):
            apart = lane - order[k]
            inv_v[...] += (k - inv_v[...]) * (1 - jnp.minimum(jnp.maximum(apart, -apart), 1))

        to_s = pltpu.make_async_copy(inv_v, inv_s, ls.at[KT + 2])
        to_s.start()
        for s in range(16):
            A[s][ZERO] = jnp.zeros((T, T), jnp.bfloat16)
        out[...] = jnp.zeros_like(out)
        to_s.wait()
        local[KT].wait()
        local[KT + 1].wait()

    for step in ORDER:
        what, *which = step.split()
        if what == "S":
            send(which[0])
        elif what == "W":
            wait(which[0])
        elif what == "E":
            expand(int(which[0]))
        elif what == "prep":
            prepare()
        elif what == "prep2":
            prepare_rest()
        elif what == "L":
            left_part(*map(int, which))
        else:
            right_part(*map(int, which))
    for c in started:
        c.wait_send()


def local_step(amplitudes, integrals, screen_mask, tile_order):
    n = len(IDS)
    scratch = [pltpu.VMEM((CAP + 1, T, T), jnp.bfloat16)] * 16 + [pltpu.SMEM((64,), jnp.int32)] * 16
    scratch += [
        pltpu.VMEM((KT * ROWT, T, T), jnp.bfloat16),
        pltpu.VMEM((64, M, T), jnp.bfloat16),
        pltpu.VMEM((8 * DEPTH, T, H), jnp.bfloat16),
        pltpu.VMEM((8 * DEPTH, T, H), jnp.bfloat16),
        pltpu.VMEM((8, 128), jnp.int32),
        pltpu.SMEM((8, 128), jnp.int32),
        pltpu.SMEM((KT * ROWT + 2,), jnp.int32),
        pltpu.SMEM((KT * ROWT + 2,), jnp.int32),
        pltpu.SMEM((KT * ROWT + 2,), jnp.int32),
        pltpu.SemaphoreType.DMA((n,)),
        pltpu.SemaphoreType.DMA((n,)),
        pltpu.SemaphoreType.DMA((KT + 3,)),
    ]
    anywhere = pl.BlockSpec(memory_space=pl.ANY)
    scalars = pl.BlockSpec(memory_space=pltpu.SMEM)
    return pl.pallas_call(
        kernel,
        out_shape=pltpu.VMEM((M, 2 * H), jnp.float32),
        in_specs=[anywhere, anywhere, scalars, scalars],
        out_specs=pl.BlockSpec(memory_space=pltpu.VMEM),
        scratch_shapes=scratch,
        cost_estimate=pl.CostEstimate(flops=2 * M * 512 * 8192, bytes_accessed=6 << 20, transcendentals=0),
        compiler_params=pltpu.CompilerParams(
            collective_id=0, has_side_effects=True, vmem_limit_bytes=58 << 20
        ),
    )(amplitudes.reshape(ROWT, T, KT * T), integrals.reshape(DEPTH, T, 2 * H), screen_mask.T, tile_order)


def solution(mesh):
    placed = (P("row", "col"), P("row", "col"), P("row", "col"), P())
    return jax.shard_map(
        local_step, mesh=mesh, in_specs=placed, out_specs=P("row", "col"), check_vma=False
    )
```

```python
import jax
import jax.numpy as jnp
from jax import lax
from jax.experimental import pallas as pl
from jax.experimental.pallas import tpu as pltpu
from jax.sharding import PartitionSpec as P

MESH = pl.DeviceIdType.MESH
T = 128
ROWT, KT, CAP = 12, 4, 24
M = ROWT * T
DEPTH = 8
H = 256
LATE = (10, 14)
ZERO = CAP
CHUNK = 768

TRANSFERS = {
    "0U1": ("u", (0, 3), 0, 4),
    "0U2": ("u", (0, 3), 4, 4),
    "0D1": ("d", (0, 1), 4, 4),
    "0D2": ("d", (0, 1), 0, 4),
    "0Z1": ("z", (1, 0), 0, 4),
    "0Z2": ("z", (1, 0), 4, 4),
    "0FU": ("u", (0, 2), 0, 4),
    "0FD": ("d", (0, 2), 4, 4),
    "0PU1": ("u", (1, 3), 0, 4),
    "0PD1": ("d", (1, 1), 4, 4),
    "0PU2": ("u", (1, 3), 4, 2),
    "0PD2": ("d", (1, 1), 2, 2),
    "0ZU": ("z", (1, 3), 6, 2),
    "0ZD": ("z", (1, 1), 0, 2),
    "0GU": ("u", (1, 2), 0, 4),
    "0GD": ("d", (1, 2), 4, 4),
    "XR1": ("r", (0, 0, 3), 0, 12),
    "XR2": ("r", (0, 0, 3), 12, 12),
    "XL1": ("l", (0, 0, 1), 12, 12),
    "XL2": ("l", (0, 0, 1), 0, 12),
    "XFR": ("r", (0, 0, 2), 0, 12),
    "XFL": ("l", (0, 0, 2), 12, 12),
    "XS0": ("s", (0, 1, 0), 0, 24),
    "XS3": ("s", (0, 1, 3), 0, 24),
    "XS1": ("s", (0, 1, 1), 0, 24),
    "XT2": ("s", (0, 1, 2), 0, 12),
    "XU2": ("s", (0, 1, 2), 12, 12),
    "YR1": ("r", (1, 0, 3), 0, 12),
    "YR2": ("r", (1, 0, 3), 12, 12),
    "YL1": ("l", (1, 0, 1), 12, 12),
    "YL2": ("l", (1, 0, 1), 0, 12),
    "YFR": ("r", (1, 0, 2), 0, 12),
    "YFL": ("l", (1, 0, 2), 12, 12),
    "YS0": ("s", (1, 1, 0), 0, 24),
    "YS3": ("s", (1, 1, 3), 0, 24),
    "YS1": ("s", (1, 1, 1), 0, 24),
    "YT2": ("s", (1, 1, 2), 0, 12),
    "YU2": ("s", (1, 1, 2), 12, 12),
    "H1": ("z", (1, 0, 0), 0, 12),
    "H2": ("z", (1, 0, 0), 12, 12),
    "1U1": ("u", (0, 3), 0, 4),
    "1U2": ("u", (0, 3), 4, 4),
    "1D1": ("d", (0, 1), 4, 4),
    "1D2": ("d", (0, 1), 0, 4),
    "1Z1": ("z", (1, 0), 0, 4),
    "1Z2": ("z", (1, 0), 4, 4),
    "1FU": ("u", (0, 2), 0, 4),
    "1FD": ("d", (0, 2), 4, 4),
    "1PU1": ("u", (1, 3), 0, 4),
    "1PD1": ("d", (1, 1), 4, 4),
    "1ZU": ("z", (1, 3), 4, 4),
    "1ZD": ("z", (1, 1), 0, 4),
    "1GU": ("u", (1, 2), 0, 4),
    "1GD": ("d", (1, 2), 4, 4),
}
ORDER = [
    "S 0Z1", "S 0U1", "S 0D1", "prep", "S XL1", "S XR1", "S XS0", "S 0U2", "S 0Z2", "S H1", "W XS0", "S 1D1", "S 1U1",
    "W 0Z1", "S H2", "S XR2", "S 0PD2", "S XL2", "W 0D1", "S 0D2", "W 0Z2", "S 1Z1", "S 0PD1", "S 1D2", "W 0U2",
    "prep2", "S 1Z2", "S 0PU2", "W XR1", "W XL1", "W 0U1", "W 1D1", "S 1U2", "S XFR", "S XFL", "W XL2", "S XS1",
    "S 0ZU", "W XR2", "S 0PU1", "S XS3", "W XS1", "E 0", "W H1", "S YL2", "S 0FU", "S YR1", "W XS3", "W 0D2",
    "W 0PD1", "W 0PD2", "W 0PU2", "W XFL", "S XU2", "S 0FD", "S 0GD", "W XFR", "S XT2", "W H2", "S YS0", "S 0ZD",
    "S YL1", "E 3", "S YR2", "W 0PU1", "W 1U1", "E 8", "S 0GU", "W 1Z1", "W YR1", "W XU2", "S 1PU1", "W 1D2", "W YS0",
    "E 12", "W 0FD", "W XT2", "E 6", "W YL2", "S 1ZD", "E 7", "S 1FU", "E 5", "S YFR", "W 1Z2", "S 1PD1", "S 1FD",
    "E 2", "W 0GU", "W 0FU", "W YL1", "S YFL", "S YS1", "W 1U2", "E 9", "W YR2", "E 11", "S YS3", "S 1ZU", "E 1",
    "E 4", "W 0GD", "W 0ZU", "W 0ZD", "L 0.6.11.3", "L 7.2.9.12", "W 1PD1", "S 1GD", "W YS1", "E 13", "W YS3",
    "W 1PU1", "E 15", "S 1GU", "L 4.15.5.13", "R 6.7.0.1", "W YFR", "S YT2", "R 8.9.2.3", "W 1ZD", "W 1FU", "W YT2",
    "W 1FD", "W YFL", "S YU2", "R 10.11.4.5", "W YU2", "W 1ZU", "R 14.15", "E 10", "E 14", "L 8.1.14.10", "W 1GD",
    "W 1GU", "R 12.16.17.13",
]
FIRST = [step[0] for step in ORDER].index("L")
IDS = {}
for _n, _t in TRANSFERS.items():
    IDS[_n] = len(IDS)
    if len(_t[1]) == 3 and _t[2] == 0:
        IDS["m" + _n] = len(IDS)


def kernel(a_in, b_in, mask, order, out, *scratch):
    A = scratch[0:16]
    meta = scratch[16:32]
    (a_loc, dense, late, b0, b1, inv_v, inv_s, nxt, pos, cnt, ss, rs, ls) = scratch[32:]
    B = (b0, b1)
    row, col = lax.axis_index("row"), lax.axis_index("col")
    y, zl = lax.rem(row, 4), lax.div(row, 4)
    core, zh, x = lax.rem(col, 2), lax.rem(lax.div(col, 2), 2), lax.div(col, 4)

    def at(dx=0, dy=0, dzl=0, dzh=0, dcore=0):
        r = lax.rem(zl + dzl, 2) * 4 + lax.rem(y + dy, 4)
        c = (lax.rem(x + dx, 4) * 2 + lax.rem(zh + dzh, 2)) * 2 + lax.rem(core + dcore, 2)
        return r, c

    up, down, zpart = at(dy=1), at(dy=3), at(dzl=1)
    right, left, hpart, sib = at(dx=1), at(dx=3), at(dzh=1), at(dcore=1)
    peers = (up, down, zpart, right, left, hpart, sib)

    barrier = pltpu.get_barrier_semaphore()
    for p in peers:
        pl.semaphore_signal(barrier, inc=1, device_id=p, device_id_type=MESH)

    local = []
    for k in range(KT):
        local.append(pltpu.make_async_copy(a_in.at[:, :, pl.ds(k * T, T)], a_loc.at[pl.ds(k * ROWT, ROWT)], ls.at[k]))
    for h in (0, 1):
        local.append(pltpu.make_async_copy(b_in.at[:, :, pl.ds(h * H, H)], B[h].at[pl.ds(row * DEPTH, DEPTH)], ls.at[KT + h]))
    for c in local[KT:] + local[:KT]:
        c.start()
    nxt[KT * ROWT] = 0

    @pl.loop(0, KT * ROWT)
    def _(n):
        t = KT * ROWT - 1 - n
        keep = mask[lax.div(t, ROWT), lax.rem(t, ROWT)]
        nxt[t] = keep * t + (1 - keep) * nxt[t + 1]

    cnt[0] = 0

    @pl.loop(0, KT * ROWT)
    def _(t):
        keep = mask[lax.div(t, ROWT), lax.rem(t, ROWT)]
        meta[0][t] = keep * cnt[t] + (1 - keep) * ZERO
        cnt[t + 1] = cnt[t] + keep

    local[KT].wait()
    local[KT + 1].wait()
    pl.semaphore_wait(barrier, len(peers))

    started = {}

    def start(i, src, dst, device):
        c = pltpu.make_async_remote_copy(src, dst, ss.at[i], rs.at[i], device_id=device, device_id_type=MESH)
        c.start()
        started[i] = c

    def drain(names):
        for n in names:
            for i in (IDS[n], IDS.get("m" + n)):
                if i in started:
                    started.pop(i).wait_send()

    def arrived(i, ref):
        pltpu.make_async_remote_copy(ref, ref, ss.at[i], rs.at[i], device_id=sib, device_id_type=MESH).wait_recv()

    def slot(dzh, dcore, dx):
        return dzh * 8 + dcore * 4 + dx

    def block(h, dzl, dy, first, count):
        r = lax.rem(zl + dzl, 2) * 4 + lax.rem(y + dy, 4)
        return B[h].at[pl.ds(r * DEPTH + first, count)]

    def send(name):
        way, land, first, count = TRANSFERS[name]
        if len(land) == 2:
            h, (dzl, dy) = int(name[0]), land
            dzl, dy = {"u": (dzl, dy + 1), "d": (dzl, dy + 3), "z": (1 - dzl, dy)}[way]
            dst = block(h, dzl, dy % 4, first, count)
            start(IDS[name], dst, dst, {"u": up, "d": down, "z": zpart}[way])
        else:
            dzh, dcore, dx = land
            frm = {"r": (dzh, dcore, dx + 1), "l": (dzh, dcore, dx + 3),
                   "z": (1 - dzh, dcore, dx), "s": (dzh, 1 - dcore, dx)}[way]
            frm, to = slot(frm[0], frm[1], frm[2] % 4), slot(*land)
            device = {"r": right, "l": left, "z": hpart, "s": sib}[way]
            tiles = pl.ds(first, count)
            start(IDS[name], A[frm].at[tiles], A[to].at[tiles], device)
            if first == 0:
                start(IDS["m" + name], meta[frm], meta[to], device)

    def wait(name):
        _, land, first, count = TRANSFERS[name]
        if len(land) == 2:
            arrived(IDS[name], block(int(name[0]), *land, first, count))
        else:
            s = slot(*land)
            arrived(IDS[name], A[s].at[pl.ds(first, count)])
            if first == 0:
                arrived(IDS["m" + name], meta[s])

    def col_of(s):
        dzh, dcore, dx = s // 8, s // 4 % 2, s % 4
        return at(dx=dx, dzh=dzh, dcore=dcore)[1]

    def place(s):
        if s in LATE:
            return late.at[pl.ds(LATE.index(s) * KT, KT)]
        return dense.at[pl.ds(col_of(s) * KT, KT)]

    def expand(s):
        to = place(s)

        @pl.loop(0, KT)
        def _(j):
            for i in range(ROWT):
                to[j, pl.ds(i * T, T), :] = A[s][meta[s][j * ROWT + i]]

    def add(half, left_tiles, right_tiles):
        rhs = jnp.concatenate(right_tiles, axis=0)
        for m in range(M // CHUNK):
            rows = pl.ds(m * CHUNK, CHUNK)
            lhs = jnp.concatenate([ref[k, rows, :] for ref, k in left_tiles], axis=1)
            out[rows, pl.ds(half * H, H)] += jnp.dot(lhs, rhs, preferred_element_type=jnp.float32)

    def panel(s, b):
        c = col_of(s) * KT
        return [(place(s), j) for j in range(KT)], [b[order[c + j]] for j in range(KT)]

    def left_part(slots):
        parts = [panel(s, b0) for s in slots]
        add(0, sum((p[0] for p in parts), []), sum((p[1] for p in parts), []))

    def right_part(quads):
        lefts, rights = [], []
        for q in quads:
            if q >= 16:
                p = panel(LATE[q - 16], b1)
                lefts, rights = lefts + p[0], rights + p[1]
                continue
            tile = at(dzl=q // 8, dy=q // 2 % 4)[0] * DEPTH + q % 2 * 4
            lefts += [(dense, inv_s[0, tile + j]) for j in range(4)]
            rights += [b1[tile + j] for j in range(4)]
        add(1, lefts, rights)

    def prepare():
        for k in range(KT):
            local[k].wait()
        pos[0] = nxt[0]

        @pl.loop(0, CAP)
        def _(s):
            A[0][s] = a_loc[pos[s]]
            pos[s + 1] = nxt[pos[s] + 1]

    def prepare_rest():
        lane = lax.broadcasted_iota(jnp.int32, (8, 128), 1)
        inv_v[...] = jnp.zeros((8, 128), jnp.int32)

        @pl.loop(0, 64)
        def _(k):
            apart = lane - order[k]
            inv_v[...] += (k - inv_v[...]) * (1 - jnp.minimum(jnp.maximum(apart, -apart), 1))

        to_s = pltpu.make_async_copy(inv_v, inv_s, ls.at[KT + 2])
        to_s.start()
        for s in range(16):
            A[s][ZERO] = jnp.zeros((T, T), jnp.bfloat16)
        out[...] = jnp.zeros_like(out)
        for s in LATE:
            dense[pl.ds(col_of(s) * KT, KT)] = jnp.zeros((KT, M, T), jnp.bfloat16)
        to_s.wait()

    waited = []
    last = [i for i, step in enumerate(ORDER) if step[0] == "W"][-1]
    for i, step in enumerate(ORDER):
        what, *which = step.split()
        if what == "S":
            send(which[0])
        elif what == "W":
            if i < FIRST or i == last:
                drain(waited[:-4])
            wait(which[0])
            waited.append(which[0])
        elif what == "E":
            expand(int(which[0]))
        elif what == "prep":
            prepare()
        elif what == "prep2":
            prepare_rest()
        elif what == "L":
            left_part([int(n) for n in which[0].split(".")])
        else:
            right_part([int(n) for n in which[0].split(".")])
    drain(waited)


def local_step(amplitudes, integrals, screen_mask, tile_order):
    n = len(IDS)
    scratch = [pltpu.VMEM((CAP + 1, T, T), jnp.bfloat16)] * 16 + [pltpu.SMEM((64,), jnp.int32)] * 16
    scratch += [
        pltpu.VMEM((KT * ROWT, T, T), jnp.bfloat16),
        pltpu.VMEM((64, M, T), jnp.bfloat16),
        pltpu.VMEM((2 * KT, M, T), jnp.bfloat16),
        pltpu.VMEM((8 * DEPTH, T, H), jnp.bfloat16),
        pltpu.VMEM((8 * DEPTH, T, H), jnp.bfloat16),
        pltpu.VMEM((8, 128), jnp.int32),
        pltpu.SMEM((8, 128), jnp.int32),
        pltpu.SMEM((KT * ROWT + 2,), jnp.int32),
        pltpu.SMEM((KT * ROWT + 2,), jnp.int32),
        pltpu.SMEM((KT * ROWT + 2,), jnp.int32),
        pltpu.SemaphoreType.DMA((n,)),
        pltpu.SemaphoreType.DMA((n,)),
        pltpu.SemaphoreType.DMA((KT + 3,)),
    ]
    anywhere = pl.BlockSpec(memory_space=pl.ANY)
    scalars = pl.BlockSpec(memory_space=pltpu.SMEM)
    return pl.pallas_call(
        kernel,
        out_shape=pltpu.VMEM((M, 2 * H), jnp.float32),
        in_specs=[anywhere, anywhere, scalars, scalars],
        out_specs=pl.BlockSpec(memory_space=pltpu.VMEM),
        scratch_shapes=scratch,
        cost_estimate=pl.CostEstimate(flops=2 * M * 512 * 8192, bytes_accessed=6 << 20, transcendentals=0),
        compiler_params=pltpu.CompilerParams(
            collective_id=0, has_side_effects=True, vmem_limit_bytes=58 << 20
        ),
    )(amplitudes.reshape(ROWT, T, KT * T), integrals.reshape(DEPTH, T, 2 * H), screen_mask.T, tile_order)


def solution(mesh):
    placed = (P("row", "col"), P("row", "col"), P("row", "col"), P())
    return jax.shard_map(
        local_step, mesh=mesh, in_specs=placed, out_specs=P("row", "col"), check_vma=False
    )
```
